1024 devices in a mesh: wide: 64 (over z, x_lo, core), narrow: 16 (over x_hi, y).
Axes of the slice: x: 4 (x_hi: 2, x_lo: 2; x = x_hi * 2 + x_lo), y: 8, z: 16, core: 2. Of those that a mesh axis runs over, the one named last changes fastest.
Arguments:
- image_emb: bfloat16 [131072, 1152], P(('wide', 'narrow')), may hold values from -0.1875 to 0.1875
- text_feat: bfloat16 [131072, 1152], P(('wide', 'narrow')), may hold values from -0.75 to 0.75
- text_head: bfloat16 [1152, 1152], replicated, may hold values from -0.1875 to 0.1875
- row_counts: int32 [1024], P(('wide', 'narrow')), may hold values from 1 to 128, 81920 in all
- positive: int32 [131072], P(('wide', 'narrow')), may hold values from 0 to 127
- log_scale: float32 [1], replicated, may hold values from 2.5 to 4
- logit_bias: float32 [1], replicated, may hold values from -3 to -1
Outputs:
- image_grad: bfloat16 [131072, 1152], P(('wide', 'narrow'))
- text_grad: bfloat16 [131072, 1152], P(('wide', 'narrow'))
- head_grad: float32 [1152, 1152], P('narrow', 'wide')
- loss: float32 [1], replicated
The draws below stay inside these ranges and needn't reach their ends.
Inputs may be any that keep to these rules, and one draw needn't show every extreme that they name: `row_counts`: live image rows of each block come first; some device has all 128 live.
All inputs are finite; a program needn't handle non-finite values.
Results may differ from the reference program's by a relative error of at most 0.0072.
Values may be sent and summed in bfloat16 or wider, within the bound.
A program may use at most 32 MiB of HBM per device.

```python
import math
import jax
import jax.numpy as jnp
import numpy as np
from jax import lax

D = 1152
ROWS = 128
TOTAL = 131072
N_WIDE = 64
N_NARROW = 16
DEVICES = 1024


def set_ends(values, stream_key, smallest, top_value):
    place = [jax.random.randint(jax.random.fold_in(stream_key, axis), (), 0, length) for axis, length in enumerate(values.shape)]
    widest = values.shape.index(max(values.shape))
    next_to = place[:widest] + [(place[widest] + 1) % values.shape[widest]] + place[widest + 1:]
    return values.at[tuple(place)].set(smallest).at[tuple(next_to)].set(top_value)


def strengthened(values, rng, source, target, parts, factor):
    def block_of(dim):
        return (jnp.arange(values.shape[dim]) // (values.shape[dim] // parts)).reshape((-1,) + (1,) * (values.ndim - 1 - dim))

    near = jax.random.permutation(rng, parts)[block_of(target)]
    far = (block_of(target) + parts // 2) % parts
    return jnp.where((block_of(source) == near) | (block_of(source) == far), factor * values, values)


def shard_levels(own_key, dims, cuts, smallest, high):
    def one(axis_at, blocks):
        heights = jax.random.uniform(jax.random.fold_in(jax.random.fold_in(own_key, 6), axis_at), (blocks,), jnp.float32, smallest / len(cuts), high / len(cuts))
        return jnp.repeat(jnp.exp(heights), dims[axis_at] // blocks).reshape((-1,) + (1,) * (len(dims) - axis_at - 1))

    gain = one(*cuts[0])
    for cut in cuts[1:]:
        gain = gain * one(*cut)
    return gain


def profile(number_of, total, bound, skew):
    weights = [(1 << 20) // math.isqrt(grade ** skew) + 1 for grade in range(2, number_of + 1)]
    rest, given = total - bound - (number_of - 1), [1] * (number_of - 1)
    while rest > 0:
        movable = [i for i in range(number_of - 1) if given[i] < bound]
        pool, left = sum([weights[i] for i in movable]), rest
        for i in movable:
            more = min(bound - given[i], max(1, left * weights[i] // pool), rest)
            given[i] = given[i] + more
            rest = rest - more
    return np.array([bound] + given)


def uneven(key, amount, total, most, slope):
    if amount == 2:
        one = jax.random.randint(key, (), max(1, total - most), min(most, total - 1) + 1)
        return jnp.stack([one, total - one])
    sizes = jnp.asarray(profile(amount, total, most, slope), jnp.int32)
    pairs = (amount - 1) // 2
    giver, receiver = sizes[1:1 + 2 * pairs:2], sizes[2:2 + 2 * pairs:2]
    slack = jnp.minimum(giver - 1, most - receiver)
    moved = jax.random.randint(jax.random.fold_in(key, 1), (pairs,), 0, 1 << 20) % (slack + 1)
    sizes = sizes.at[1:1 + 2 * pairs:2].set(giver - moved).at[2:2 + 2 * pairs:2].set(receiver + moved)
    return sizes[jax.random.permutation(jax.random.fold_in(key, 2), amount)]


def bell_draw(own_key, dims, scale, reach, shards=(), kind=jnp.bfloat16):
    loudness = shard_levels(own_key, dims, shards, -0.22, 0.18) if shards else 1.0
    array = jax.random.normal(own_key, dims, jnp.float32) * scale * loudness
    return jnp.minimum(jnp.maximum(array, -reach), reach).astype(kind)


def gaussian_with(stream_key, shape, width, reach, pieces, heavy, kind=jnp.bfloat16):
    values = width * jax.random.normal(stream_key, shape, jnp.float32)
    if pieces:
        values = values * shard_levels(stream_key, shape, pieces, -0.22, 0.18)
    return jnp.clip(strengthened(values, jax.random.fold_in(stream_key, 3), *heavy), -reach, reach).astype(kind)


def setup_inputs(seed: int = 0) -> dict:
    key_of = jax.random.split(jax.random.key(seed), 8)
    return {
        "image_emb": bell_draw(key_of[0], (TOTAL, D), 0.03, 0.1875, ((0, 1024),)),
        "text_feat": gaussian_with(key_of[1], (TOTAL, D), 0.03, 0.75, ((0, 1024),), (0, 1, 128, 5.5)),
        "text_head": bell_draw(key_of[2], (D, D), D ** -0.5, 0.1875),
        "row_counts": uneven(key_of[3], DEVICES, DEVICES * ROWS * 5 // 8, ROWS, 1).astype(jnp.int32),
        "positive": set_ends(jax.random.randint(key_of[4], (TOTAL,), 0, ROWS), jax.random.fold_in(key_of[4], 1), 0, ROWS - 1).astype(jnp.int32),
        "log_scale": jnp.clip(jax.random.uniform(key_of[5], (1,), jnp.float32, 2.5, 4.0), 2.5, 4.0),
        "logit_bias": jnp.clip(jax.random.uniform(key_of[6], (1,), jnp.float32, -3.0, -1.0), -3.0, -1.0),
    }


EPSILON = 1e-06

def unit_rows(values):
    row_norms = jnp.sqrt(lax.optimization_barrier(jnp.sum(values * values, axis=-1, keepdims=True)) + EPSILON)
    return (values / row_norms, row_norms)

def rounded_copy(values):
    return lax.optimization_barrier(values.astype(jnp.bfloat16)).astype(jnp.float32)

def reference(image_emb, text_feat, text_head, row_counts, positive, log_scale, logit_bias):
    devices = N_WIDE * N_NARROW
    logit_scale = jnp.exp(log_scale[0])
    offset_value = logit_bias[0]
    image_unit, image_norm = unit_rows(image_emb.astype(jnp.float32))
    image_blocks = rounded_copy(image_unit).reshape(devices, ROWS, D)
    projected = jnp.dot(text_feat, text_head, preferred_element_type=jnp.float32)
    text_unit, text_norm = unit_rows(projected)
    text_blocks = rounded_copy(text_unit).reshape(devices, ROWS, D)
    device_ids = jnp.arange(devices, dtype=jnp.int32)
    near_ids = device_ids ^ N_NARROW // 2
    far_ids = device_ids ^ devices // 2
    diag_ids = near_ids ^ devices // 2
    row_ids = jnp.arange(ROWS, dtype=jnp.int32)
    valid_rows = (row_ids[None, :] < row_counts[:, None]).astype(jnp.float32)[:, :, None]
    own_sign = jnp.where(row_ids[None, None, :] == positive.reshape(devices, ROWS)[:, :, None], 1.0, -1.0).astype(jnp.float32)
    weight_scale = logit_scale / ROWS

    def score_tile(partner_blocks, label_sign):
        logits = logit_scale * jnp.einsum('dik,djk->dij', image_blocks, partner_blocks) + offset_value
        losses = jnp.sum(jax.nn.softplus(-label_sign * logits) * valid_rows)
        weights = rounded_copy(-label_sign * jax.nn.sigmoid(-label_sign * logits) * valid_rows * weight_scale)
        image_part = jnp.einsum('dij,djk->dik', weights, partner_blocks)
        text_part = jnp.einsum('dij,dik->djk', weights, image_blocks)
        return (losses, image_part, text_part)
    own_loss, image_dir, text_dir = score_tile(text_blocks, own_sign)
    loss_total = own_loss
    for partner_ids in (near_ids, far_ids, diag_ids):
        tile_loss, image_part, text_part = score_tile(text_blocks[partner_ids], jnp.float32(-1.0))
        loss_total = loss_total + tile_loss
        image_dir = image_dir + image_part
        text_dir = text_dir + rounded_copy(text_part)[partner_ids]
    image_dir = image_dir.reshape(devices * ROWS, D)
    text_dir = text_dir.reshape(devices * ROWS, D)
    image_along = lax.optimization_barrier(jnp.sum(image_unit * image_dir, axis=-1, keepdims=True))
    image_grad = ((image_dir - image_unit * image_along) / image_norm).astype(jnp.bfloat16)
    text_along = lax.optimization_barrier(jnp.sum(text_unit * text_dir, axis=-1, keepdims=True))
    text_step = ((text_dir - text_unit * text_along) / text_norm).astype(jnp.bfloat16)
    text_grad = jnp.dot(text_step, text_head.T, preferred_element_type=jnp.float32).astype(jnp.bfloat16)
    head_grad = jnp.dot(text_feat.T, text_step, preferred_element_type=jnp.float32)
    loss = (loss_total / (ROWS * devices)).reshape(1).astype(jnp.float32)
    return (image_grad, text_grad, head_grad, loss)
```

```python
import jax
import jax.numpy as jnp
from jax import lax
from jax.experimental import pallas as pl
from jax.experimental.pallas import tpu as pltpu
from jax.sharding import PartitionSpec as P

EPSILON = 1e-06
VMEM_BYTES = int(53.2 * 2**20)
MESH = pl.DeviceIdType.MESH
F32 = jnp.float32
BF16 = jnp.bfloat16

ROWS = 128
WIDTH = 1152
N_Z = 16
N_Y = 8
N_X = 4
DEVICES = 1024
CHUNKS = 4
CHUNK = ROWS // CHUNKS
HALF = WIDTH // 2
QUARTER = WIDTH // 4
OUT_ROWS = WIDTH // 16
OUT_COLS = WIDTH // 64
Y_PAD = 80
Z_PAD = 32
STEP_ROWS = QUARTER + 16

X_PEERS = [(dx, dc) for dx in (2, 1, 3, 0) for dc in range(2) if (dx, dc) != (0, 0)]


def position():
    wide, narrow = lax.axis_index("wide"), lax.axis_index("narrow")
    return {
        "z": wide // 4,
        "x": (narrow // N_Y) * 2 + (wide // 2) % 2,
        "core": wide % 2,
        "y": narrow % N_Y,
    }


def moved(pos, dz=0, dy=0, dx=0, dc=0):
    return {
        "z": (pos["z"] + dz) % N_Z,
        "y": (pos["y"] + dy) % N_Y,
        "x": (pos["x"] + dx) % N_X,
        "core": (pos["core"] + dc) % 2,
    }


def flipped(pos, bit):
    return dict(pos, z=pos["z"] + bit - 2 * bit * ((pos["z"] // bit) % 2))


def device_of(pos):
    return (
        pos["z"] * 4 + (pos["x"] % 2) * 2 + pos["core"],
        (pos["x"] // 2) * N_Y + pos["y"],
    )


def nt(left, right):
    return lax.dot_general(left, right, (((1,), (1,)), ((), ())), preferred_element_type=F32)


def tn(left, right):
    return lax.dot_general(left, right, (((0,), (0,)), ((), ())), preferred_element_type=F32)


def thirds(value):
    high = value.astype(BF16).astype(F32)
    middle = (value - high).astype(BF16).astype(F32)
    low = value - high - middle
    row = lax.broadcasted_iota(jnp.int32, (8, ROWS), 0)
    return jnp.where(row == 0, high, jnp.where(row == 1, middle, jnp.where(row == 2, low, 0.0)))


def whole(rows):
    return jnp.sum(rows, axis=0, keepdims=True)


def nn(left, right):
    return jnp.dot(left, right, preferred_element_type=F32)


def kernel(
    image_in, feat_in, head_in, positive_in, counts_ref, log_scale_ref, bias_ref,
    image_grad_ref, text_grad_ref, head_grad_ref, loss_ref,
    image_ref, feat_ref, head_ref, positive_ref,
    image_own, text_own, image_near, text_near, image_far, text_far, image_diag, text_diag,
    text_unit, text_dir, image_dir, feat_t, feat_all, step_t, step_q, step_out, step_all,
    head_part, y_send, y_recv, z_part, z_send, z_recv,
    send_sem, recv_sem, local_sem, round_sem,
):
    loads = [
        pltpu.make_async_copy(source, target, local_sem.at[2 + i])
        for i, (source, target) in enumerate(
            [
                (image_in, image_ref),
                (feat_in, feat_ref),
                (head_in, head_ref),
                (positive_in, positive_ref),
            ]
        )
    ]
    for load in loads:
        load.start()
    pos = position()
    peers = {"far": moved(pos, dz=8), "near": moved(pos, dx=2)}
    barrier = pltpu.get_barrier_semaphore()
    greeted = (
        [flipped(pos, bit) for bit in (8, 4, 2, 1)]
        + [moved(pos, dy=dy) for dy in range(1, N_Y)]
        + [moved(pos, dx=dx, dc=dc) for dx, dc in X_PEERS]
    )
    for peer in greeted:
        pl.semaphore_signal(barrier, inc=1, device_id=device_of(peer), device_id_type=MESH)

    used = []

    def send(source, target, peer):
        slot = len(used)
        copy = pltpu.make_async_remote_copy(
            src_ref=source,
            dst_ref=target,
            send_sem=send_sem.at[slot],
            recv_sem=recv_sem.at[slot],
            device_id=device_of(peer),
            device_id_type=MESH,
        )
        copy.start()
        used.append(copy)
        return copy

    def tell(bit):
        pl.semaphore_signal(
            round_sem.at[bit // 2], inc=1, device_id=device_of(flipped(pos, bit)), device_id_type=MESH
        )

    def told(bit):
        pl.semaphore_wait(round_sem.at[bit // 2], 1)

    def arrived(copies):
        for copy in copies:
            copy.wait_recv()

    scale = jnp.exp(jnp.full((1, 1), log_scale_ref[0], F32))
    bias = jnp.full((1, 1), bias_ref[0], F32)
    weight_scale = scale / ROWS
    count = counts_ref[0]
    live_rows = lax.broadcasted_iota(jnp.int32, (ROWS, 1), 0) < count
    live_lanes = (lax.broadcasted_iota(jnp.int32, (1, ROWS), 1) < count).astype(F32)

    def image_rows():
        rows = image_ref[...].astype(F32)
        norm = jnp.sqrt(jnp.sum(rows * rows, axis=-1, keepdims=True) + EPSILON)
        return rows / norm, norm

    loads[0].wait()
    image_own[...] = jnp.where(live_rows, image_rows()[0], 0.0).astype(BF16)

    pl.semaphore_wait(barrier, len(greeted))

    def chunk(ref, index):
        return ref.at[pl.ds(index * CHUNK, CHUNK)]

    image_out = [send(chunk(image_own, i), chunk(image_far, i), peers["far"]) for i in range(CHUNKS)]
    image_near_copy = send(image_own, image_near, peers["near"])

    tell(1)

    loads[1].wait()
    feat_t[...] = jnp.transpose(feat_ref[...].astype(F32)).astype(BF16)
    own_lanes = pl.ds(pl.multiple_of((pos["x"] * 2 + pos["core"]) * ROWS, ROWS), ROWS)

    def feat_rows(peer):
        return feat_t.at[pl.ds(pl.multiple_of((peer["x"] // 2) * HALF, HALF), HALF)]

    feat_copies = []
    for dx, dc in X_PEERS:
        peer = moved(pos, dx=dx, dc=dc)
        feat_copies.append(send(feat_rows(peer), feat_all.at[:, own_lanes], peer))
    own_feat = pltpu.make_async_copy(feat_rows(pos), feat_all.at[:, own_lanes], local_sem.at[0])
    own_feat.start()

    y_send[...] = jnp.zeros(y_send.shape, BF16)
    z_part[...] = jnp.zeros(z_part.shape, F32)
    loads[2].wait()
    projected = nn(feat_ref[...], head_ref[...])
    text_norm = jnp.sqrt(jnp.sum(projected * projected, axis=-1, keepdims=True) + EPSILON)
    text_unit[...] = projected / text_norm
    text_own[...] = text_unit[...].astype(BF16)
    text_near_copy = send(text_own, text_near, peers["near"])

    def tile(text, image, sign):
        logits = scale * nt(text, image) + bias
        turned = -sign * logits
        decay = jnp.exp(-jnp.abs(turned))
        losses = jnp.maximum(turned, 0.0) + jnp.log1p(decay)
        weights = -sign * (jnp.where(turned >= 0, 1.0, decay) / (1.0 + decay)) * weight_scale
        return losses, weights

    def total(values):
        return jnp.sum(jnp.sum(values, axis=0, keepdims=True), axis=1, keepdims=True)

    loads[3].wait()
    matches = lax.broadcasted_iota(jnp.int32, (ROWS, ROWS), 0) == positive_ref[...]
    losses, weights = tile(text_own[...], image_own[...], jnp.where(matches, 1.0, -1.0).astype(F32))
    local_loss = total(losses * live_lanes)
    weights = (weights * live_lanes).astype(BF16)
    text_dir[...] = nn(weights, image_own[...])
    image_dir[...] = tn(weights, text_own[...])

    def text_side(image):
        losses, weights = tile(text_own[...], image[...], -1.0)
        text_dir[...] += nn(weights.astype(BF16), image[...])
        return total(losses)

    def image_side(text):
        _, weights = tile(text[...], image_own[...], -1.0)
        image_dir[...] += tn((weights * live_lanes).astype(BF16), text[...])

    arrived([image_near_copy])
    local_loss += text_side(image_near)
    arrived([text_near_copy])
    image_side(text_near)

    image_diag_copies, text_out = [], []
    for i in range(CHUNKS):
        arrived([image_out[i]])
        image_diag_copies.append(send(chunk(image_far, i), chunk(image_diag, i), peers["near"]))
        text_out.append(send(chunk(text_own, i), chunk(text_far, i), peers["far"]))
    local_loss += text_side(image_far)
    arrived(image_diag_copies)
    local_loss += text_side(image_diag)
    dead_loss = jnp.maximum(bias, 0.0) + jnp.log1p(jnp.exp(-jnp.abs(bias)))
    dead_pairs = (3 * ROWS * (ROWS - jnp.full((1, 1), count, jnp.int32))).astype(F32)
    local_loss -= dead_loss * dead_pairs

    direction = text_dir[...]
    along = jnp.sum(text_unit[...] * direction, axis=-1, keepdims=True)
    step = ((direction - text_unit[...] * along) / text_norm).astype(BF16)
    step_t[...] = jnp.transpose(step.astype(F32))
    for quarter in range(4):
        for z in range(N_Z):
            step_q[quarter * QUARTER + z * OUT_COLS : quarter * QUARTER + (z + 1) * OUT_COLS, :] = step_t[
                (z * 4 + quarter) * OUT_COLS : (z * 4 + quarter + 1) * OUT_COLS, :
            ]
    loss_rows = jnp.concatenate([thirds(local_loss), jnp.zeros((STEP_ROWS - QUARTER - 8, ROWS), F32)], axis=0)
    for quarter in range(4):
        start = quarter * STEP_ROWS
        step_out[start : start + QUARTER, :] = step_q[quarter * QUARTER : (quarter + 1) * QUARTER, :].astype(BF16)
        step_out[start + QUARTER : start + STEP_ROWS, :] = loss_rows.astype(BF16)

    def step_rows(peer):
        quarter = (peer["x"] % 2) * 2 + peer["core"]
        return step_out.at[pl.ds(pl.multiple_of(quarter * STEP_ROWS, STEP_ROWS), STEP_ROWS)]

    step_copies = []
    for dx, dc in X_PEERS:
        peer = moved(pos, dx=dx, dc=dc)
        step_copies.append(send(step_rows(peer), step_all.at[:, own_lanes], peer))
    own_step = pltpu.make_async_copy(step_rows(pos), step_all.at[:, own_lanes], local_sem.at[1])
    own_step.start()

    text_grad_ref[...] = nt(step, head_ref[...]).astype(BF16)
    told(1)
    tell(2)

    arrived(feat_copies)
    own_feat.wait()
    arrived(step_copies)
    own_step.wait()
    head_part[...] = nt(feat_all[...], step_all[0:QUARTER, :])
    parts = step_all[QUARTER:STEP_ROWS, :].astype(F32)
    line_loss = thirds(sum(whole(parts[:, i * ROWS : (i + 1) * ROWS]) for i in range(8))[:, 0:1])
    y_copies = []
    for slot, dy in enumerate(sorted(range(1, N_Y), key=lambda d: -min(d, N_Y - d))):
        peer = moved(pos, dy=dy)
        rows = head_part[pl.ds(pl.multiple_of(peer["y"] * OUT_ROWS, OUT_ROWS), OUT_ROWS), :]
        y_send[slot, 0:OUT_ROWS, :] = rows.astype(BF16)
        y_send[slot, OUT_ROWS:Y_PAD, 0:ROWS] = line_loss.astype(BF16)
        y_copies.append(send(y_send.at[slot], y_recv.at[slot], peer))
    told(2)
    tell(4)
    text_diag_copies = []
    for i in range(CHUNKS):
        arrived([text_out[i]])
        text_diag_copies.append(send(chunk(text_far, i), chunk(text_diag, i), peers["near"]))

    arrived(y_copies)
    rows = head_part[pl.ds(pl.multiple_of(pos["y"] * OUT_ROWS, OUT_ROWS), OUT_ROWS), :]
    for index in range(N_Y - 1):
        rows += y_recv[index, 0:OUT_ROWS, :].astype(F32)
        line_loss += y_recv[index, OUT_ROWS:Y_PAD, 0:ROWS].astype(F32)
    plane_loss = thirds(whole(line_loss)[:, 0:1])
    rows = jnp.concatenate([rows, jnp.zeros((OUT_ROWS, 3 * ROWS - QUARTER), F32)], axis=1)
    rows = jnp.concatenate([rows, jnp.zeros((ROWS - OUT_ROWS, 3 * ROWS), F32)], axis=0)
    step_t[0 : 3 * ROWS, :] = jnp.transpose(rows)
    for z in range(N_Z):
        z_part[z, 0:OUT_COLS, :] = step_t[z * OUT_COLS : (z + 1) * OUT_COLS, :]
        z_part[z, OUT_COLS : OUT_COLS + 3, :] = plane_loss[0:3, :]
    z_send[...] = z_part[...].astype(BF16)

    told(4)
    z_copies = []
    for dz in sorted(range(1, N_Z), key=lambda d: -min(d, N_Z - d)):
        peer = moved(pos, dz=dz)
        z_copies.append(send(z_send.at[peer["z"]], z_recv.at[dz - 1], peer))

    image_side(text_far)
    arrived(text_diag_copies)
    image_side(text_diag)
    unit, norm = image_rows()
    direction = image_dir[...]
    along = jnp.sum(unit * direction, axis=-1, keepdims=True)
    image_grad_ref[...] = ((direction - unit * along) / norm).astype(BF16)

    arrived(z_copies)
    block = z_part[pos["z"]]
    for index in range(N_Z - 1):
        block += z_recv[index].astype(F32)
    head_grad_ref[...] = block[0:OUT_COLS, 0:OUT_ROWS]
    loss_ref[...] = whole(block[OUT_COLS : OUT_COLS + 3, 0:1]) / (ROWS * DEVICES)
    for copy in used:
        copy.wait_send()


COPIES = 2 * CHUNKS * 2 + 2 + 2 * len(X_PEERS) + (N_Y - 1) + (N_Z - 1)


def per_device(image_emb, text_feat, text_head, row_counts, positive, log_scale, logit_bias):
    vmem = pl.BlockSpec(memory_space=pltpu.VMEM)
    smem = pl.BlockSpec(memory_space=pltpu.SMEM)
    hbm = pl.BlockSpec(memory_space=pltpu.HBM)
    block = pltpu.VMEM((ROWS, WIDTH), BF16)
    wide_block = pltpu.VMEM((ROWS, WIDTH), F32)
    image_grad, text_grad, head_grad, loss = pl.pallas_call(
        kernel,
        name="sigmoid_loss_step",
        out_shape=(
            jax.ShapeDtypeStruct((ROWS, WIDTH), BF16),
            jax.ShapeDtypeStruct((ROWS, WIDTH), BF16),
            jax.ShapeDtypeStruct((OUT_COLS, OUT_ROWS), F32),
            jax.ShapeDtypeStruct((1, 1), F32),
        ),
        in_specs=[hbm, hbm, hbm, hbm, smem, smem, smem],
        out_specs=(vmem, vmem, vmem, vmem),
        scratch_shapes=[block, block, pltpu.VMEM((WIDTH, WIDTH), BF16), pltpu.VMEM((1, ROWS), jnp.int32)]
        + [block] * 8
        + [wide_block] * 3
        + [
            pltpu.VMEM((WIDTH, ROWS), BF16),
            pltpu.VMEM((HALF, 8 * ROWS), BF16),
            pltpu.VMEM((WIDTH, ROWS), F32),
            pltpu.VMEM((WIDTH, ROWS), F32),
            pltpu.VMEM((4 * STEP_ROWS, ROWS), BF16),
            pltpu.VMEM((STEP_ROWS, 8 * ROWS), BF16),
            pltpu.VMEM((HALF, QUARTER), F32),
            pltpu.VMEM((N_Y - 1, Y_PAD, QUARTER), BF16),
            pltpu.VMEM((N_Y - 1, Y_PAD, QUARTER), BF16),
            pltpu.VMEM((N_Z, Z_PAD, ROWS), F32),
            pltpu.VMEM((N_Z, Z_PAD, ROWS), BF16),
            pltpu.VMEM((N_Z - 1, Z_PAD, ROWS), BF16),
            pltpu.SemaphoreType.DMA((COPIES,)),
            pltpu.SemaphoreType.DMA((COPIES,)),
            pltpu.SemaphoreType.DMA((6,)),
            pltpu.SemaphoreType.REGULAR((3,)),
        ],
        compiler_params=pltpu.CompilerParams(
            collective_id=0, has_side_effects=True, vmem_limit_bytes=VMEM_BYTES
        ),
    )(image_emb, text_feat, text_head, positive.reshape(1, ROWS), row_counts, log_scale, logit_bias)
    return image_grad, text_grad, head_grad.T, loss.reshape(1)


def solution(mesh):
    rows = P(("wide", "narrow"), None)
    blocks = P(("wide", "narrow"))
    return jax.shard_map(
        per_device,
        mesh=mesh,
        in_specs=(rows, rows, P(), blocks, blocks, P(), P()),
        out_specs=(rows, rows, P("narrow", "wide"), P()),
        check_vma=False,
    )
```

```python
import jax
import jax.numpy as jnp
from jax import lax
from jax.experimental import pallas as pl
from jax.experimental.pallas import tpu as pltpu
from jax.sharding import PartitionSpec as P

EPSILON = 1e-06
VMEM_BYTES = int(53.2 * 2**20)
MESH = pl.DeviceIdType.MESH
F32 = jnp.float32
BF16 = jnp.bfloat16

ROWS = 128
WIDTH = 1152
N_Z = 16
N_Y = 8
N_X = 4
DEVICES = 1024
CHUNKS = 4
CHUNK = ROWS // CHUNKS
HALF = WIDTH // 2
QUARTER = WIDTH // 4
OUT_ROWS = WIDTH // 16
OUT_COLS = WIDTH // 64
Y_PAD = 80
Z_PAD = 16
STEP_ROWS = QUARTER + 16

X_PEERS = [(dx, dc) for dx in (2, 1, 3, 0) for dc in range(2) if (dx, dc) != (0, 0)]


def position():
    wide, narrow = lax.axis_index("wide"), lax.axis_index("narrow")
    return {
        "z": wide // 4,
        "x": (narrow // N_Y) * 2 + (wide // 2) % 2,
        "core": wide % 2,
        "y": narrow % N_Y,
    }


def moved(pos, dz=0, dy=0, dx=0, dc=0):
    return {
        "z": (pos["z"] + dz) % N_Z,
        "y": (pos["y"] + dy) % N_Y,
        "x": (pos["x"] + dx) % N_X,
        "core": (pos["core"] + dc) % 2,
    }


def flipped(pos, bit):
    return dict(pos, z=pos["z"] + bit - 2 * bit * ((pos["z"] // bit) % 2))


def device_of(pos):
    return (
        pos["z"] * 4 + (pos["x"] % 2) * 2 + pos["core"],
        (pos["x"] // 2) * N_Y + pos["y"],
    )


def nt(left, right):
    return lax.dot_general(left, right, (((1,), (1,)), ((), ())), preferred_element_type=F32)


def tn(left, right):
    return lax.dot_general(left, right, (((0,), (0,)), ((), ())), preferred_element_type=F32)


def thirds(value):
    high = value.astype(BF16).astype(F32)
    middle = (value - high).astype(BF16).astype(F32)
    low = value - high - middle
    row = lax.broadcasted_iota(jnp.int32, (8, ROWS), 0)
    return jnp.where(row == 0, high, jnp.where(row == 1, middle, jnp.where(row == 2, low, 0.0)))


def whole(rows):
    return jnp.sum(rows, axis=0, keepdims=True)


def nn(left, right):
    return jnp.dot(left, right, preferred_element_type=F32)


def kernel(
    image_in, feat_in, head_in, positive_in, counts_ref, log_scale_ref, bias_ref,
    image_grad_ref, text_grad_ref, head_grad_ref, loss_ref,
    image_ref, feat_ref, head_ref, positive_ref,
    image_own, text_own, image_near, text_near, image_far, text_far, image_diag, text_diag,
    text_unit, text_dir, image_dir, feat_t, feat_all, step_t, step_q, step_out, step_all,
    head_part, y_send, y_recv, z_part, z_send, z_recv,
    send_sem, recv_sem, local_sem, round_sem,
):
    loads = [
        pltpu.make_async_copy(source, target, local_sem.at[2 + i])
        for i, (source, target) in enumerate(
            [
                (image_in, image_ref),
                (feat_in, feat_ref),
                (head_in, head_ref),
                (positive_in, positive_ref),
            ]
        )
    ]
    for load in loads:
        load.start()
    pos = position()
    peers = {"far": moved(pos, dz=8), "near": moved(pos, dx=2)}
    barrier = pltpu.get_barrier_semaphore()
    greeted = (
        [flipped(pos, bit) for bit in (8, 4, 2, 1)]
        + [moved(pos, dy=dy) for dy in range(1, N_Y)]
        + [moved(pos, dx=dx, dc=dc) for dx, dc in X_PEERS]
    )
    for peer in greeted:
        pl.semaphore_signal(barrier, inc=1, device_id=device_of(peer), device_id_type=MESH)

    used = []

    def send(source, target, peer):
        slot = len(used)
        copy = pltpu.make_async_remote_copy(
            src_ref=source,
            dst_ref=target,
            send_sem=send_sem.at[slot],
            recv_sem=recv_sem.at[slot],
            device_id=device_of(peer),
            device_id_type=MESH,
        )
        copy.start()
        used.append(copy)
        return copy

    def tell(bit):
        pl.semaphore_signal(
            round_sem.at[bit // 2], inc=1, device_id=device_of(flipped(pos, bit)), device_id_type=MESH
        )

    def told(bit):
        pl.semaphore_wait(round_sem.at[bit // 2], 1)

    def arrived(copies):
        for copy in copies:
            copy.wait_recv()

    scale = jnp.exp(jnp.full((1, 1), log_scale_ref[0], F32))
    bias = jnp.full((1, 1), bias_ref[0], F32)
    weight_scale = scale / ROWS
    count = counts_ref[0]
    live_rows = lax.broadcasted_iota(jnp.int32, (ROWS, 1), 0) < count
    live_lanes = (lax.broadcasted_iota(jnp.int32, (1, ROWS), 1) < count).astype(F32)

    def image_rows():
        rows = image_ref[...].astype(F32)
        norm = jnp.sqrt(jnp.sum(rows * rows, axis=-1, keepdims=True) + EPSILON)
        return rows / norm, norm

    loads[0].wait()
    image_own[...] = jnp.where(live_rows, image_rows()[0], 0.0).astype(BF16)

    pl.semaphore_wait(barrier, len(greeted))

    def chunk(ref, index):
        return ref.at[pl.ds(index * CHUNK, CHUNK)]

    image_out = [send(chunk(image_own, i), chunk(image_far, i), peers["far"]) for i in range(CHUNKS)]
    image_near_copy = send(image_own, image_near, peers["near"])

    tell(1)

    loads[1].wait()
    feat_t[...] = jnp.transpose(feat_ref[...].astype(F32)).astype(BF16)
    own_lanes = pl.ds(pl.multiple_of((pos["x"] * 2 + pos["core"]) * ROWS, ROWS), ROWS)

    def feat_rows(peer):
        return feat_t.at[pl.ds(pl.multiple_of((peer["x"] // 2) * HALF, HALF), HALF)]

    feat_copies = []
    for dx, dc in X_PEERS:
        peer = moved(pos, dx=dx, dc=dc)
        feat_copies.append(send(feat_rows(peer), feat_all.at[:, own_lanes], peer))
    own_feat = pltpu.make_async_copy(feat_rows(pos), feat_all.at[:, own_lanes], local_sem.at[0])
    own_feat.start()

    y_send[...] = jnp.zeros(y_send.shape, BF16)
    loads[2].wait()
    projected = nn(feat_ref[...], head_ref[...])
    text_norm = jnp.sqrt(jnp.sum(projected * projected, axis=-1, keepdims=True) + EPSILON)
    text_unit[...] = projected / text_norm
    text_own[...] = text_unit[...].astype(BF16)
    text_near_copy = send(text_own, text_near, peers["near"])

    def tile(text, image, sign):
        logits = scale * nt(text, image) + bias
        turned = -sign * logits
        decay = jnp.exp(-jnp.abs(turned))
        losses = jnp.maximum(turned, 0.0) + jnp.log1p(decay)
        weights = -sign * (jnp.where(turned >= 0, 1.0, decay) / (1.0 + decay)) * weight_scale
        return losses, weights

    def total(values):
        return jnp.sum(jnp.sum(values, axis=0, keepdims=True), axis=1, keepdims=True)

    loads[3].wait()
    matches = lax.broadcasted_iota(jnp.int32, (ROWS, ROWS), 0) == positive_ref[...]
    losses, weights = tile(text_own[...], image_own[...], jnp.where(matches, 1.0, -1.0).astype(F32))
    local_loss = total(losses * live_lanes)
    weights = (weights * live_lanes).astype(BF16)
    text_dir[...] = nn(weights, image_own[...])
    image_dir[...] = tn(weights, text_own[...])

    def text_side(image):
        losses, weights = tile(text_own[...], image[...], -1.0)
        text_dir[...] += nn(weights.astype(BF16), image[...])
        return total(losses)

    def image_side(text):
        _, weights = tile(text[...], image_own[...], -1.0)
        image_dir[...] += tn((weights * live_lanes).astype(BF16), text[...])

    arrived([image_near_copy])
    local_loss += text_side(image_near)
    arrived([text_near_copy])
    image_side(text_near)

    image_diag_copies, text_out = [], []
    for i in range(CHUNKS):
        arrived([image_out[i]])
        image_diag_copies.append(send(chunk(image_far, i), chunk(image_diag, i), peers["near"]))
        text_out.append(send(chunk(text_own, i), chunk(text_far, i), peers["far"]))
    local_loss += text_side(image_far)
    arrived(image_diag_copies)
    local_loss += text_side(image_diag)
    dead_loss = jnp.maximum(bias, 0.0) + jnp.log1p(jnp.exp(-jnp.abs(bias)))
    dead_pairs = (3 * ROWS * (ROWS - jnp.full((1, 1), count, jnp.int32))).astype(F32)
    local_loss -= dead_loss * dead_pairs

    direction = text_dir[...]
    along = jnp.sum(text_unit[...] * direction, axis=-1, keepdims=True)
    step = ((direction - text_unit[...] * along) / text_norm).astype(BF16)
    step_t[...] = jnp.transpose(step.astype(F32))
    for quarter in range(4):
        for z in range(N_Z):
            step_q[quarter * QUARTER + z * OUT_COLS : quarter * QUARTER + (z + 1) * OUT_COLS, :] = step_t[
                (z * 4 + quarter) * OUT_COLS : (z * 4 + quarter + 1) * OUT_COLS, :
            ]
    loss_rows = jnp.concatenate([thirds(local_loss), jnp.zeros((STEP_ROWS - QUARTER - 8, ROWS), F32)], axis=0)
    for quarter in range(4):
        start = quarter * STEP_ROWS
        step_out[start : start + QUARTER, :] = step_q[quarter * QUARTER : (quarter + 1) * QUARTER, :].astype(BF16)
        step_out[start + QUARTER : start + STEP_ROWS, :] = loss_rows.astype(BF16)

    def step_rows(peer):
        quarter = (peer["x"] % 2) * 2 + peer["core"]
        return step_out.at[pl.ds(pl.multiple_of(quarter * STEP_ROWS, STEP_ROWS), STEP_ROWS)]

    step_copies = []
    for dx, dc in X_PEERS:
        peer = moved(pos, dx=dx, dc=dc)
        step_copies.append(send(step_rows(peer), step_all.at[:, own_lanes], peer))
    own_step = pltpu.make_async_copy(step_rows(pos), step_all.at[:, own_lanes], local_sem.at[1])
    own_step.start()

    text_grad_ref[...] = nt(step, head_ref[...]).astype(BF16)
    told(1)
    tell(2)

    arrived(feat_copies)
    own_feat.wait()
    arrived(step_copies)
    own_step.wait()
    head_part[...] = nt(feat_all[...], step_all[0:QUARTER, :])
    parts = step_all[QUARTER:STEP_ROWS, :].astype(F32)
    line_loss = thirds(sum(whole(parts[:, i * ROWS : (i + 1) * ROWS]) for i in range(8))[:, 0:1])
    y_copies = []
    for slot, dy in enumerate(sorted(range(1, N_Y), key=lambda d: -min(d, N_Y - d))):
        peer = moved(pos, dy=dy)
        rows = head_part[pl.ds(pl.multiple_of(peer["y"] * OUT_ROWS, OUT_ROWS), OUT_ROWS), :]
        y_send[slot, 0:OUT_ROWS, :] = rows.astype(BF16)
        y_send[slot, OUT_ROWS:Y_PAD, 0:ROWS] = line_loss.astype(BF16)
        y_copies.append(send(y_send.at[slot], y_recv.at[slot], peer))
    told(2)
    tell(4)
    text_diag_copies = []
    for i in range(CHUNKS):
        arrived([text_out[i]])
        text_diag_copies.append(send(chunk(text_far, i), chunk(text_diag, i), peers["near"]))

    arrived(y_copies)
    rows = head_part[pl.ds(pl.multiple_of(pos["y"] * OUT_ROWS, OUT_ROWS), OUT_ROWS), :]
    for index in range(N_Y - 1):
        rows += y_recv[index, 0:OUT_ROWS, :].astype(F32)
        line_loss += y_recv[index, OUT_ROWS:Y_PAD, 0:ROWS].astype(F32)
    plane_loss = thirds(whole(line_loss)[:, 0:1])
    rows = jnp.concatenate([rows, jnp.zeros((OUT_ROWS, 3 * ROWS - QUARTER), F32)], axis=1)
    rows = jnp.concatenate([rows, jnp.zeros((ROWS - OUT_ROWS, 3 * ROWS), F32)], axis=0)
    step_t[0 : 3 * ROWS, :] = jnp.transpose(rows)
    lane = lax.broadcasted_iota(jnp.int32, (8, ROWS), 1)
    row = lax.broadcasted_iota(jnp.int32, (8, ROWS), 0)
    loss_rows = pltpu.roll(plane_loss, 4, 0)
    for z in range(N_Z):
        start = z * OUT_COLS
        last = step_t[start + 16 : start + 24, :]
        front = pltpu.roll(last, OUT_ROWS, 1)
        back = pltpu.roll(pltpu.roll(last, OUT_ROWS // 2, 1), 2, 0)
        spare = jnp.where(row < 2, front, jnp.where(row < 4, back, loss_rows))
        z_part[z, 0:8, :] = jnp.where(lane < OUT_ROWS, step_t[start : start + 8, :], spare)
        z_part[z, 8:16, :] = step_t[start + 8 : start + 16, :]
    z_send[...] = z_part[...].astype(BF16)

    told(4)
    z_copies = []
    for dz in sorted(range(1, N_Z), key=lambda d: -min(d, N_Z - d)):
        peer = moved(pos, dz=dz)
        z_copies.append(send(z_send.at[peer["z"]], z_recv.at[dz - 1], peer))

    image_side(text_far)
    arrived(text_diag_copies)
    image_side(text_diag)
    unit, norm = image_rows()
    direction = image_dir[...]
    along = jnp.sum(unit * direction, axis=-1, keepdims=True)
    image_grad_ref[...] = ((direction - unit * along) / norm).astype(BF16)

    arrived(z_copies)
    block = z_part[pos["z"]]
    for index in range(N_Z - 1):
        block += z_recv[index].astype(F32)
    first = block[0:8, :]
    front = pltpu.roll(first, ROWS - OUT_ROWS, 1)
    back = pltpu.roll(pltpu.roll(first, ROWS - OUT_ROWS // 2, 1), 6, 0)
    last = jnp.where(lane < OUT_ROWS // 2, front, back)
    head_grad_ref[0:16, :] = block[:, 0:OUT_ROWS]
    head_grad_ref[16:OUT_COLS, :] = last[0 : OUT_COLS - 16, 0:OUT_ROWS]
    loss_ref[...] = whole(first[4:7, ROWS - 1 : ROWS]) / (ROWS * DEVICES)
    for copy in used:
        copy.wait_send()


COPIES = 2 * CHUNKS * 2 + 2 + 2 * len(X_PEERS) + (N_Y - 1) + (N_Z - 1)


def per_device(image_emb, text_feat, text_head, row_counts, positive, log_scale, logit_bias):
    vmem = pl.BlockSpec(memory_space=pltpu.VMEM)
    smem = pl.BlockSpec(memory_space=pltpu.SMEM)
    hbm = pl.BlockSpec(memory_space=pltpu.HBM)
    block = pltpu.VMEM((ROWS, WIDTH), BF16)
    wide_block = pltpu.VMEM((ROWS, WIDTH), F32)
    image_grad, text_grad, head_grad, loss = pl.pallas_call(
        kernel,
        name="sigmoid_loss_step",
        out_shape=(
            jax.ShapeDtypeStruct((ROWS, WIDTH), BF16),
            jax.ShapeDtypeStruct((ROWS, WIDTH), BF16),
            jax.ShapeDtypeStruct((OUT_COLS, OUT_ROWS), F32),
            jax.ShapeDtypeStruct((1, 1), F32),
        ),
        in_specs=[hbm, hbm, hbm, hbm, smem, smem, smem],
        out_specs=(vmem, vmem, vmem, vmem),
        scratch_shapes=[block, block, pltpu.VMEM((WIDTH, WIDTH), BF16), pltpu.VMEM((1, ROWS), jnp.int32)]
        + [block] * 8
        + [wide_block] * 3
        + [
            pltpu.VMEM((WIDTH, ROWS), BF16),
            pltpu.VMEM((HALF, 8 * ROWS), BF16),
            pltpu.VMEM((WIDTH, ROWS), F32),
            pltpu.VMEM((WIDTH, ROWS), F32),
            pltpu.VMEM((4 * STEP_ROWS, ROWS), BF16),
            pltpu.VMEM((STEP_ROWS, 8 * ROWS), BF16),
            pltpu.VMEM((HALF, QUARTER), F32),
            pltpu.VMEM((N_Y - 1, Y_PAD, QUARTER), BF16),
            pltpu.VMEM((N_Y - 1, Y_PAD, QUARTER), BF16),
            pltpu.VMEM((N_Z, Z_PAD, ROWS), F32),
            pltpu.VMEM((N_Z, Z_PAD, ROWS), BF16),
            pltpu.VMEM((N_Z - 1, Z_PAD, ROWS), BF16),
            pltpu.SemaphoreType.DMA((COPIES,)),
            pltpu.SemaphoreType.DMA((COPIES,)),
            pltpu.SemaphoreType.DMA((6,)),
            pltpu.SemaphoreType.REGULAR((3,)),
        ],
        compiler_params=pltpu.CompilerParams(
            collective_id=0, has_side_effects=True, vmem_limit_bytes=VMEM_BYTES
        ),
    )(image_emb, text_feat, text_head, positive.reshape(1, ROWS), row_counts, log_scale, logit_bias)
    return image_grad, text_grad, head_grad.T, loss.reshape(1)


def solution(mesh):
    rows = P(("wide", "narrow"), None)
    blocks = P(("wide", "narrow"))
    return jax.shard_map(
        per_device,
        mesh=mesh,
        in_specs=(rows, rows, P(), blocks, blocks, P(), P()),
        out_specs=(rows, rows, P("narrow", "wide"), P()),
        check_vma=False,
    )
```
